32 devices in a mesh: seq: 8 (over z, y), ep: 4 (over x, core).
Axes of the slice: x: 2, y: 2, z: 4, core: 2. Of those that a mesh axis runs over, the one named last changes fastest.
Arguments:
- queries: bfloat16 [3072, 6144], P('seq', 'ep'), may hold values from -5 to 5
- key_heads: bfloat16 [3072, 1024], P('seq', 'ep'), may hold values from -4 to 4, as said below
- value_heads: bfloat16 [3072, 1024], P('seq', 'ep'), may hold values from -6 to 6, as said below
- attn_grad: bfloat16 [3072, 6144], P('seq', 'ep'), may hold values from -6 to 6
- segments: int32 [3072], P('seq'), may hold values from 0 to 15, never falling along the last dimension, each value on 1 to 1153 neighbouring positions
- moe_grad: bfloat16 [3072, 6144], P(('seq', 'ep')), may hold values from -6 to 6
- expert_out: bfloat16 [3072, 2, 6144], P(('seq', 'ep')), may hold values from -6 to 6
- normed: bfloat16 [3072, 6144], P(('seq', 'ep')), may hold values from -6 to 6
- router: bfloat16 [8, 6144], replicated, may hold values from -0.078125 to 0.078125
- routes: int32 [3072, 2], P(('seq', 'ep')), may hold values from 0 to 7, all different within a row; in each aligned block of 96 rows (0 to 95, 96 to 191, ...) at most 24 rows name the same one
Outputs:
- query_grad: bfloat16 [3072, 6144], P('seq', 'ep')
- key_grad: bfloat16 [3072, 1024], P('seq', 'ep')
- value_grad: bfloat16 [3072, 1024], P('seq', 'ep')
- normed_grad: bfloat16 [3072, 6144], P(('seq', 'ep'))
- router_grad: float32 [8, 6144], replicated
- routed_grads: bfloat16 [128, 48, 6144], P(('seq', 'ep'))
The draws below stay inside these ranges and needn't reach their ends.
Inputs may be any that keep to these rules, and one draw needn't show every extreme that they name: `key_heads`: the 1 indices of ep e with the same e // 1 hold identical copies. `value_heads`: the 1 indices of ep e with the same e // 1 hold identical copies. `segments`: segment numbers never fall along the sequence; every document has 1 to 1153 tokens and one has exactly 1153. A token names two different experts; in each aligned block of 96 tokens (the tokens of one device) every expert is named by exactly 24 routes.
All inputs are finite; a program needn't handle non-finite values.
Results may differ from the reference program's by a relative error of at most 0.0071.
Values may be sent and summed in bfloat16 or wider, within the bound.
A program may use at most 192 MiB of HBM per device.

```python
import functools
import math
import jax
import jax.numpy as jnp
import numpy as np
from jax import lax

D = 6144
EXPERTS = 8
HD = 128
TOP = 2
REACH = 3
TOK = 384
SEQLEN = 3072
DOC_MOST = 1153
DOCS = 16
QH_DEV = 12
KV_DEV = 2
KV_SHARE = 1
GROUP = 6
MOE_DEV = 96
CAP = 24
EXP_DEV = 2
SPLIT = 1
N_SEQ = 8
N_EP = 4


def copy_heads(base):
    return jnp.repeat(base, KV_SHARE, axis=1)


def draw_key_heads(key, part):
    shape = (SEQLEN, N_EP // KV_SHARE, KV_DEV, HD)
    base = copy_heads(jax.random.truncated_normal(jax.random.fold_in(key, 3), -4.0, 4.0, shape, jnp.float32))
    return base.reshape(SEQLEN, N_EP * KV_DEV * HD).astype(jnp.bfloat16)


def draw_value_heads(key, part):
    shape = (SEQLEN, N_EP // KV_SHARE, KV_DEV, HD)
    base = jax.random.truncated_normal(jax.random.fold_in(key, 7), -6.0, 6.0, shape, jnp.float32)
    return copy_heads(base).reshape(SEQLEN, N_EP * KV_DEV * HD).astype(jnp.bfloat16)


def draw_queries(key, part):
    shape = (SEQLEN, N_EP, KV_DEV, GROUP, HD)
    base = jax.random.truncated_normal(jax.random.fold_in(key, 5), -5.0, 5.0, shape, jnp.float32)
    return base.reshape(SEQLEN, N_EP * KV_DEV * GROUP * HD).astype(jnp.bfloat16)


def steps_of(stream_key, shape, cuts, low, top_value):
    def one(axis_at, parts):
        draws = jax.random.uniform(jax.random.fold_in(jax.random.fold_in(stream_key, 6), axis_at), (parts,), jnp.float32, low / len(cuts), top_value / len(cuts))
        return jnp.repeat(jnp.exp(draws), shape[axis_at] // parts).reshape((-1,) + (1,) * (len(shape) - axis_at - 1))

    gain = one(*cuts[0])
    for cut in cuts[1:]:
        gain = gain * one(*cut)
    return gain


def split_up(amount, total, bound, lean):
    portions = [(1 << 20) // math.isqrt(standing ** lean) + 1 for standing in range(2, amount + 1)]
    surplus, holding = total - bound - (amount - 1), [1] * (amount - 1)
    while surplus > 0:
        movable = [i for i in range(amount - 1) if holding[i] < bound]
        pool, left = sum([portions[i] for i in movable]), surplus
        for i in movable:
            more = min(bound - holding[i], max(1, left * portions[i] // pool), surplus)
            holding[i] = holding[i] + more
            surplus = surplus - more
    return np.array([bound] + holding)


def ragged_sizes(key, amount, total, limit, lean):
    if amount == 2:
        one = jax.random.randint(key, (), max(1, total - limit), min(limit, total - 1) + 1)
        return jnp.stack([one, total - one])
    tallies = jnp.asarray(split_up(amount, total, limit, lean), jnp.int32)
    pairs = (amount - 1) // 2
    giver, taker = tallies[1:1 + 2 * pairs:2], tallies[2:2 + 2 * pairs:2]
    slack = jnp.minimum(giver - 1, limit - taker)
    passed = jax.random.randint(jax.random.fold_in(key, 1), (pairs,), 0, 1 << 20) % (slack + 1)
    tallies = tallies.at[1:1 + 2 * pairs:2].set(giver - passed).at[2:2 + 2 * pairs:2].set(taker + passed)
    return tallies[jax.random.permutation(jax.random.fold_in(key, 2), amount)]


def routed_block(key, own, number, rows, count, top, limit, skew):
    sequence = jax.random.permutation(key, count)
    heavy_load, common = load_shares(count, rows * top, limit, skew, True), load_shares(count, rows * top, limit, skew, False)
    places = jnp.arange(count)

    def named(lengths, offset_by):
        used = int((lengths > 0).sum())
        fixed = max(1, used // 4)
        moved = fixed + (places - fixed + offset_by * (used - fixed)) % max(1, count - fixed)
        return jnp.zeros((count,), jnp.int32).at[sequence[jnp.where(places < fixed, places, moved)]].set(jnp.asarray(lengths, jnp.int32))

    lengths = jnp.where(number % 4 == 0, named(heavy_load, number // 4), named(common, number - number // 4 - 1))
    mixed = jax.random.permutation(jax.random.fold_in(own, 3), count)
    source_of, taker = mixed[0:count // 2 * 2:2], mixed[1:count // 2 * 2:2]
    room = jnp.minimum(lengths[source_of] - 1, limit - lengths[taker]) // 2
    room = jnp.where((source_of == sequence[0]) | (taker == sequence[0]) | (lengths[taker] == 0), 0, jnp.maximum(room, 0))
    moved = jax.random.randint(jax.random.fold_in(own, 4), (count // 2,), 0, 1 << 20) % (room + 1)
    lengths = lengths.at[source_of].add(-moved).at[taker].add(moved)
    items = jnp.searchsorted(jnp.cumsum(lengths), jnp.arange(rows * top), side="right").astype(jnp.int32)
    listing = items.reshape(top, rows).T
    listing = listing[jax.random.permutation(jax.random.fold_in(own, 1), rows)]
    offset_by = jax.random.randint(jax.random.fold_in(own, 2), (rows, 1), 0, top)
    return jnp.take_along_axis(listing, (jnp.arange(top)[None, :] + offset_by) % top, axis=1)


def load_shares(count, total, bound, skew, full):
    weights = [(1 << 20) // math.isqrt(standing ** skew) + 1 for standing in range(1, count + 1)]
    largest = bound if full else min(bound, max(-(-total // count), total * weights[0] // sum(weights)))
    least = 1 if total - largest >= count - 1 else 0
    given, surplus = [largest] + [least] * (count - 1), total - largest - least * (count - 1)
    while surplus > 0:
        movable = [i for i in range(1, count) if given[i] < largest] or [i for i in range(1, count) if given[i] < bound]
        mass, budget = sum([weights[i] for i in movable]), surplus
        for i in movable:
            addition = min(bound - given[i], max(1, budget * weights[i] // mass), surplus)
            given[i] = given[i] + addition
            surplus = surplus - addition
    return np.array(given)


def centred(stream_key, shape, scale, most, pieces=(), kind=jnp.bfloat16):
    values = jax.random.normal(stream_key, shape, jnp.float32) * scale
    if len(pieces) > 0:
        values = steps_of(stream_key, shape, pieces, -0.22, 0.18) * values
    return jnp.clip(values, min=-most, max=most).astype(kind)


def setup_inputs(seed: int = 0) -> dict:
    key_list = jax.random.split(jax.random.key(seed), 11)
    queries = draw_queries(jax.random.fold_in(key_list[10], 71), 0)
    key_heads = draw_key_heads(jax.random.fold_in(key_list[10], 71), 0)
    value_heads = draw_value_heads(jax.random.fold_in(key_list[10], 71), 0)
    attn_grad = centred(key_list[3], (SEQLEN, N_EP * QH_DEV * HD), 1.0, 6.0, ((0, 8), (1, 4)))
    segments = jnp.searchsorted(jnp.cumsum(ragged_sizes(key_list[4], DOCS, SEQLEN, DOC_MOST, 1)), jnp.arange(SEQLEN), side="right").astype(jnp.int32)
    moe_grad = centred(key_list[5], (SEQLEN, D), 1.0, 6.0, ((0, 32),))
    expert_out = centred(key_list[6], (SEQLEN, TOP, D), 1.0, 6.0, ((0, 32),))
    normed = centred(key_list[7], (SEQLEN, D), 1.0, 6.0, ((0, 32),))
    router = centred(key_list[8], (EXPERTS, D), D ** -0.5, 0.078125)
    routes_keys = jax.random.split(jax.random.fold_in(key_list[9], 1), SEQLEN // MOE_DEV)
    routes_turns = jax.random.permutation(jax.random.fold_in(key_list[9], 3), SEQLEN // MOE_DEV)
    routes = jax.vmap(lambda own, number: routed_block(jax.random.fold_in(key_list[9], 2), own, number, MOE_DEV, EXPERTS, TOP, CAP, 0))(routes_keys, routes_turns).reshape((SEQLEN, TOP))
    return {"queries": queries, "key_heads": key_heads, "value_heads": value_heads, "attn_grad": attn_grad, "segments": segments, "moe_grad": moe_grad, "expert_out": expert_out, "normed": normed, "router": router, "routes": routes}


MASKED = -1e+30

def attention_grads(queries, key_heads, value_heads, attn_grad, segments):
    score_scale = 1.0 / math.sqrt(HD)
    num_blocks = SEQLEN // TOK
    query_all = queries.astype(jnp.float32).reshape(num_blocks, TOK, N_EP, KV_DEV, GROUP, HD)
    grad_all = attn_grad.astype(jnp.float32).reshape(num_blocks, TOK, N_EP, KV_DEV, GROUP, HD)
    key_all = key_heads.astype(jnp.float32).reshape(num_blocks, TOK, N_EP, KV_DEV, HD)
    value_all = value_heads.astype(jnp.float32).reshape(num_blocks, TOK, N_EP, KV_DEV, HD)
    seg_all = segments.reshape(num_blocks, TOK)
    positions = jnp.arange(TOK, dtype=jnp.int32)

    def allowed(row_block, col_block):
        clipped = jnp.maximum(col_block, 0)
        row_pos = row_block * TOK + positions
        col_pos = col_block * TOK + positions
        same_doc = seg_all[row_block][:, None] == seg_all[clipped][None, :]
        return same_doc & (col_pos[None, :] <= row_pos[:, None]) & (col_block >= 0)

    def is_live(row_block, col_block):
        clipped = jnp.maximum(col_block, 0)
        return (col_block >= 0) & (seg_all[clipped][TOK - 1] >= seg_all[row_block][0])

    def scores_and_grad(row_block, col_block):
        clipped = jnp.maximum(col_block, 0)
        mask = allowed(row_block, col_block)
        raw_scores = jnp.einsum('qehgd,tehd->ehgqt', query_all[row_block], key_all[clipped]) * score_scale
        scores = jnp.where(mask, raw_scores, MASKED)
        prob_grad = jnp.einsum('qehgd,tehd->ehgqt', grad_all[row_block], value_all[clipped])
        return (mask, scores, prob_grad)

    def stats_block(row_block, col_block, running):
        row_peak, row_total, weighted = running
        mask, scores, prob_grad = scores_and_grad(row_block, col_block)
        new_peak = jnp.maximum(row_peak, lax.optimization_barrier(jnp.max(scores, axis=-1)))
        factor = jnp.exp(row_peak - new_peak)
        weights = jnp.where(mask, jnp.exp(scores - new_peak[..., None]), 0.0)
        return (new_peak, row_total * factor + lax.optimization_barrier(jnp.sum(weights, axis=-1)), weighted * factor + lax.optimization_barrier(jnp.sum(weights * prob_grad, axis=-1)))

    def grad_block(row_block, col_block, log_total, delta, carried):
        query_acc, key_acc, value_acc = carried
        clipped = jnp.maximum(col_block, 0)
        mask, scores, prob_grad = scores_and_grad(row_block, col_block)
        soft_probs = jnp.where(mask, jnp.exp(scores - log_total[..., None]), 0.0)
        probs_low = lax.optimization_barrier(soft_probs.astype(jnp.bfloat16)).astype(jnp.float32)
        value_part = jnp.einsum('ehgqt,qehgd->tehd', probs_low, grad_all[row_block])
        score_low = lax.optimization_barrier((soft_probs * (prob_grad - delta[..., None])).astype(jnp.bfloat16)).astype(jnp.float32)
        query_part = jnp.einsum('ehgqt,tehd->qehgd', score_low, key_all[clipped]) * score_scale
        key_part = jnp.einsum('ehgqt,qehgd->tehd', score_low, query_all[row_block]) * score_scale
        return (query_acc + query_part, key_acc.at[clipped].add(key_part), value_acc.at[clipped].add(value_part))

    def scan_step(carried, row_block):
        key_acc, value_acc = carried
        stat_shape = (N_EP, KV_DEV, GROUP, TOK)
        running = (jnp.full(stat_shape, MASKED, jnp.float32), jnp.zeros(stat_shape, jnp.float32), jnp.zeros(stat_shape, jnp.float32))
        for offset in range(REACH + 1):
            col_block = row_block - offset
            running = lax.cond(is_live(row_block, col_block), functools.partial(stats_block, row_block, col_block), lambda unchanged: unchanged, running)
        row_peak, row_total, weighted = running
        log_total = row_peak + jnp.log(row_total)
        delta = weighted / row_total
        accs = (jnp.zeros((TOK, N_EP, KV_DEV, GROUP, HD), jnp.float32), key_acc, value_acc)
        for offset in range(REACH + 1):
            col_block = row_block - offset
            accs = lax.cond(is_live(row_block, col_block), functools.partial(grad_block, row_block, col_block, log_total, delta), lambda unchanged: unchanged, accs)
        return ((accs[1], accs[2]), accs[0])
    zero_keys = jnp.zeros((num_blocks, TOK, N_EP, KV_DEV, HD), jnp.float32)
    (key_acc, value_acc), query_blocks = lax.scan(scan_step, (zero_keys, zero_keys), jnp.arange(num_blocks, dtype=jnp.int32))
    query_grad = query_blocks.reshape(SEQLEN, N_EP * QH_DEV * HD).astype(jnp.bfloat16)
    key_grad = key_acc.reshape(SEQLEN, N_EP * KV_DEV * HD).astype(jnp.bfloat16)
    value_grad = value_acc.reshape(SEQLEN, N_EP * KV_DEV * HD).astype(jnp.bfloat16)
    return (query_grad, key_grad, value_grad)

def router_grads(moe_grad, expert_out, normed, router, routes):
    logits = jnp.einsum('td,ed->te', normed.astype(jnp.float32), router.astype(jnp.float32))
    expert_ids = jnp.arange(EXPERTS, dtype=jnp.int32)
    onehot = (routes[:, :, None] == expert_ids[None, None, :]).astype(jnp.float32)
    chosen = lax.optimization_barrier(jnp.sum(onehot * logits[:, None, :], axis=2))
    first_gate = 1.0 / (1.0 + jnp.exp(chosen[:, 1] - chosen[:, 0]))
    second_gate = 1.0 - first_gate
    gate_grad = jnp.einsum('td,tkd->tk', moe_grad.astype(jnp.float32), expert_out.astype(jnp.float32))
    logit_step = first_gate * second_gate * (gate_grad[:, 0] - gate_grad[:, 1])
    logit_grad = (onehot[:, 0, :] - onehot[:, 1, :]) * logit_step[:, None]
    normed_grad = jnp.dot(logit_grad, router.astype(jnp.float32), precision=lax.Precision.HIGHEST).astype(jnp.bfloat16)
    router_grad = jnp.dot(logit_grad.T, normed.astype(jnp.float32), precision=lax.Precision.HIGHEST) / SEQLEN
    gates = jnp.stack([first_gate, second_gate], axis=1)
    expert_rows = (gates[:, :, None] * moe_grad.astype(jnp.float32)[:, None, :]).astype(jnp.bfloat16)
    num_blocks = SEQLEN // MOE_DEV
    route_count = MOE_DEV * TOP
    flat_routes = routes.reshape(num_blocks, route_count)
    hot = (flat_routes[:, :, None] == expert_ids[None, None, :]).astype(jnp.int32)
    ranks = lax.optimization_barrier(jnp.sum((jnp.cumsum(hot, axis=1) - 1) * hot, axis=2))
    order = jnp.argsort(flat_routes * CAP + ranks, axis=1).astype(jnp.int32)
    global_index = order + (jnp.arange(num_blocks, dtype=jnp.int32) * route_count)[:, None]
    slot_index = global_index.reshape(N_SEQ, N_EP, EXPERTS, CAP)
    slot_index = jnp.repeat(slot_index, SPLIT, axis=2).reshape(N_SEQ, N_EP, N_EP, EXP_DEV * CAP)
    slot_index = jnp.transpose(slot_index, (0, 2, 1, 3)).reshape(N_SEQ * N_EP * N_EP, EXP_DEV * CAP)
    routed_grads = expert_rows.reshape(SEQLEN * TOP, D)[slot_index]
    return (normed_grad, router_grad, routed_grads)

def reference(queries, key_heads, value_heads, attn_grad, segments, moe_grad, expert_out, normed, router, routes):
    query_grad, key_grad, value_grad = attention_grads(queries, key_heads, value_heads, attn_grad, segments)
    normed_grad, router_grad, routed_grads = router_grads(moe_grad, expert_out, normed, router, routes)
    return (query_grad, key_grad, value_grad, normed_grad, router_grad, routed_grads)
```

```python
import functools
import math

import jax
import jax.numpy as jnp
from jax import lax
from jax.experimental import pallas as pl
from jax.experimental.pallas import tpu as pltpu
from jax.sharding import PartitionSpec as P

EXPERTS = 8
HD = 128
TOP = 2
REACH = 3
QT = 128
MASKED = -1e30
F32 = jnp.float32
BF16 = jnp.bfloat16
VMEM_LIMIT = 48 * 1024 * 1024
SCALE = 1.0 / math.sqrt(HD)
SCALE2 = SCALE * math.log2(math.e)


def from_behind(value, axis, by):
    devices = lax.axis_size(axis)
    pairs = [(i, i + by) for i in range(devices) if 0 <= i + by < devices]
    return lax.ppermute(value, axis, pairs)


def nt(a, b):
    return lax.dot_general(a, b, (((1,), (1,)), ((), ())), preferred_element_type=F32)


def nn(a, b):
    return jnp.dot(a, b, preferred_element_type=F32)


def attn_kernel(group, tok, aliased, *refs):
    if aliased:
        refs = refs[1:]
    (start_ref, q_ref, g_ref, k0, v0, k1, v1, k2, v2, k3, v3,
     dq_ref, own_ref, far_ref, kcat, vcat, kt, bias, dk, dv) = refs
    step = pl.program_id(0)
    steps = pl.num_programs(0)
    window = REACH * tok + QT

    @pl.when(step == 0)
    def _():
        for n, (k, v) in enumerate(((k3, v3), (k2, v2), (k1, v1), (k0, v0))):
            kcat[n * tok:(n + 1) * tok, :] = k[...]
            vcat[n * tok:(n + 1) * tok, :] = v[...]
            kt[:, n * tok:(n + 1) * tok] = k[...].astype(F32).T.astype(BF16)
        dk[...] = jnp.zeros_like(dk)
        dv[...] = jnp.zeros_like(dv)

    base = pl.multiple_of(step * QT, QT)
    keys = pl.ds(base, window)
    position = lax.broadcasted_iota(jnp.int32, (window, QT), 0)
    limit = REACH * tok + lax.broadcasted_iota(jnp.int32, (window, QT), 1)
    allowed = (position >= start_ref[...] - base) & (position <= limit)
    bias[...] = jnp.where(allowed, 0.0, MASKED)
    together = 2 if group % 2 == 0 else 1
    for first in range(0, group, together):
        heads = range(first, first + together)
        q = jnp.concatenate([q_ref[:, h * HD:(h + 1) * HD] for h in heads], axis=0)
        g = jnp.concatenate([g_ref[:, h * HD:(h + 1) * HD] for h in heads], axis=0)
        kwin = kcat[keys, :]
        scores = nt(kwin, q) + jnp.concatenate([bias[...]] * together, axis=1)
        prob_grad = nt(vcat[keys, :], g)
        peak = jnp.max(scores, axis=0, keepdims=True)
        weights = jnp.exp2((scores - peak) * SCALE2)
        inverse = 1.0 / jnp.sum(weights, axis=0, keepdims=True)
        delta = jnp.sum(weights * prob_grad, axis=0, keepdims=True) * inverse
        probs = weights * inverse
        score_low = (probs * (prob_grad - delta)).astype(BF16)
        dv[keys, :] += nn(probs.astype(BF16), g)
        dk[keys, :] += nn(score_low, q)
        dq = (nn(kt[:, keys], score_low) * SCALE).T.astype(BF16)
        for n, h in enumerate(heads):
            dq_ref[:, h * HD:(h + 1) * HD] = dq[n * QT:(n + 1) * QT, :]

    @pl.when(step == steps - 1)
    def _():
        own_ref[:, :HD] = dk[REACH * tok:, :] * SCALE
        own_ref[:, HD:] = dv[REACH * tok:, :]
        for n in range(REACH):
            rows = slice((REACH - 1 - n) * tok, (REACH - n) * tok)
            far_ref[n, :, :HD] = (dk[rows, :] * SCALE).astype(BF16)
            far_ref[n, :, HD:] = dv[rows, :].astype(BF16)


def attention_head(head, kv_heads, group, start, queries, attn_grad, key_heads, value_heads, far, dq_prev):
    tok = queries.shape[0]
    keys = (REACH + 1) * tok
    width = group * HD
    row_spec = pl.BlockSpec((QT, width), lambda i: (i, head))
    own_spec = pl.BlockSpec((tok, HD), lambda i: (0, head))
    far_k = pl.BlockSpec((tok, HD), lambda i: (0, head))
    far_v = pl.BlockSpec((tok, HD), lambda i: (0, kv_heads + head))
    in_specs = [pl.BlockSpec((1, QT), lambda i: (0, i)), row_spec, row_spec, own_spec, own_spec]
    args = [start, queries, attn_grad, key_heads, value_heads]
    for block in far:
        in_specs += [far_k, far_v]
        args += [block, block]
    aliases = {}
    if dq_prev is not None:
        in_specs = [pl.BlockSpec(memory_space=pl.ANY)] + in_specs
        args = [dq_prev] + args
        aliases = {0: 0}
    work = (tok // QT) * (REACH * tok + QT) * QT * group
    return pl.pallas_call(
        functools.partial(attn_kernel, group, tok, dq_prev is not None),
        grid=(tok // QT,),
        in_specs=in_specs,
        out_specs=(
            row_spec,
            pl.BlockSpec((tok, 2 * HD), lambda i: (0, 0)),
            pl.BlockSpec((REACH, tok, 2 * HD), lambda i: (0, 0, 0)),
        ),
        out_shape=(
            jax.ShapeDtypeStruct(queries.shape, BF16),
            jax.ShapeDtypeStruct((tok, 2 * HD), F32),
            jax.ShapeDtypeStruct((REACH, tok, 2 * HD), BF16),
        ),
        scratch_shapes=[
            pltpu.VMEM((keys, HD), BF16),
            pltpu.VMEM((keys, HD), BF16),
            pltpu.VMEM((HD, keys), BF16),
            pltpu.VMEM((REACH * tok + QT, QT), F32),
            pltpu.VMEM((keys, HD), F32),
            pltpu.VMEM((keys, HD), F32),
        ],
        input_output_aliases=aliases,
        compiler_params=pltpu.CompilerParams(vmem_limit_bytes=VMEM_LIMIT),
        cost_estimate=pl.CostEstimate(flops=work * HD * 10, bytes_accessed=tok * width * 6, transcendentals=work),
        name="attention",
    )(*args)


def split3(x):
    high = x.astype(BF16)
    rest = x - high.astype(F32)
    mid = rest.astype(BF16)
    low = (rest - mid.astype(F32)).astype(BF16)
    return jnp.concatenate([high.astype(F32), mid.astype(F32), low.astype(F32)], axis=0).astype(BF16)


def route_kernel(capacity, copies, all_tokens, routes_ref, moe_ref, expert_ref, normed_ref, router_ref,
                 ngrad_ref, rgrad_ref, out_ref):
    rows, width = moe_ref.shape
    slots = out_ref.shape[0]
    logits = nt(router_ref[...], normed_ref[...])
    expert = lax.broadcasted_iota(jnp.int32, (EXPERTS, rows), 0)
    e0 = routes_ref[0:1, :]
    e1 = routes_ref[1:2, :]
    hot0 = (expert == e0).astype(F32)
    hot1 = (expert == e1).astype(F32)
    chosen0 = jnp.sum(hot0 * logits, axis=0, keepdims=True)
    chosen1 = jnp.sum(hot1 * logits, axis=0, keepdims=True)
    first = 1.0 / (1.0 + jnp.exp(chosen1 - chosen0))
    second = 1.0 - first
    product = nt(expert_ref[...], moe_ref[...])
    which = lax.broadcasted_iota(jnp.int32, product.shape, 0)
    token = lax.broadcasted_iota(jnp.int32, product.shape, 1)
    signed = jnp.where(which == 2 * token, product, jnp.where(which == 2 * token + 1, -product, 0.0))
    step = first * second * jnp.sum(signed, axis=0, keepdims=True)
    pieces = split3((hot0 - hot1) * step)
    earlier = lax.broadcasted_iota(jnp.int32, (rows, rows), 0) < lax.broadcasted_iota(jnp.int32, (rows, rows), 1)
    rank = nn((hot0 + hot1).astype(BF16), earlier.astype(BF16))
    rank0 = jnp.sum(hot0 * rank, axis=0, keepdims=True).astype(jnp.int32)
    rank1 = jnp.sum(hot1 * rank, axis=0, keepdims=True).astype(jnp.int32)
    slot = lax.broadcasted_iota(jnp.int32, (slots, rows), 0)
    slot = (slot // (copies * capacity)) * capacity + slot % capacity
    take0 = slot == e0 * capacity + rank0
    take1 = slot == e1 * capacity + rank1
    gate = jnp.sum(jnp.where(take0, first, 0.0) + jnp.where(take1, second, 0.0), axis=1, keepdims=True)
    pick = (take0 | take1).astype(BF16)
    chunk = 512
    for at in range(0, width, chunk):
        columns = slice(at, at + chunk)
        out_ref[:, columns] = (nn(pick, moe_ref[:, columns]) * gate).astype(BF16)
        table = jnp.concatenate([router_ref[:, columns].astype(F32)] * 3, axis=0).astype(BF16)
        ngrad_ref[:, columns] = lax.dot_general(
            pieces, table, (((0,), (0,)), ((), ())), preferred_element_type=F32
        ).astype(BF16)
        sums = nn(pieces, normed_ref[:, columns])
        rgrad_ref[:, columns] = (
            sums[0:EXPERTS] + sums[EXPERTS:2 * EXPERTS] + sums[2 * EXPERTS:]
        ) * (1.0 / all_tokens)


def on_device(queries, key_heads, value_heads, attn_grad, segments, moe_grad, expert_out, normed, router, routes):
    tok = queries.shape[0]
    kv_heads = key_heads.shape[1] // HD
    group = queries.shape[1] // (kv_heads * HD)
    seq_index = lax.axis_index("seq")
    ep_size = lax.axis_size("ep")
    both = jnp.concatenate([key_heads, value_heads], axis=1)
    far = [from_behind(both, "seq", offset) for offset in range(1, REACH + 1)]
    behind = jnp.int32(0)
    for offset in range(1, REACH + 1):
        segs = from_behind(segments, "seq", offset)
        behind += jnp.where(seq_index >= offset, jnp.sum((segs == segments[0]).astype(jnp.int32)), 0)
    inside = jnp.sum((segments[:, None] < segments[None, :]).astype(jnp.int32), axis=0)
    start = (REACH * tok + inside - jnp.where(segments == segments[0], behind, 0))[None, :]

    moe_rows, width = moe_grad.shape
    capacity = moe_rows * TOP // EXPERTS
    copies = max(1, ep_size // EXPERTS)
    per_device = max(1, EXPERTS // ep_size)
    slots = EXPERTS * copies * capacity
    devices = lax.axis_size("seq") * ep_size
    normed_grad, local_router, outgoing = pl.pallas_call(
        functools.partial(route_kernel, capacity, copies, moe_rows * devices),
        out_shape=(
            jax.ShapeDtypeStruct((moe_rows, width), BF16),
            jax.ShapeDtypeStruct((EXPERTS, width), F32),
            jax.ShapeDtypeStruct((slots, width), BF16),
        ),
        compiler_params=pltpu.CompilerParams(vmem_limit_bytes=VMEM_LIMIT),
        cost_estimate=pl.CostEstimate(flops=8 * slots * moe_rows * width, bytes_accessed=12 * moe_rows * width, transcendentals=0),
        name="routing",
    )(routes.T, moe_grad, expert_out.reshape(TOP * moe_rows, width), normed, router)
    routed_grads = lax.all_to_all(
        outgoing.reshape(ep_size, per_device * capacity, width), "ep", split_axis=0, concat_axis=0, tiled=True
    )
    parts = lax.all_to_all(
        local_router.reshape(devices, -1), ("seq", "ep"), split_axis=0, concat_axis=0, tiled=True
    )
    total = jnp.broadcast_to(jnp.sum(parts, axis=0, keepdims=True), parts.shape)
    router_grad = lax.all_to_all(
        total, ("seq", "ep"), split_axis=0, concat_axis=0, tiled=True
    ).reshape(EXPERTS, width)

    query_grad = None
    key_parts = []
    value_parts = []
    for head in range(kv_heads):
        query_grad, own, away = attention_head(
            head, kv_heads, group, start, queries, attn_grad, key_heads, value_heads, far, query_grad
        )
        for offset in range(1, REACH + 1):
            own = own + from_behind(away[offset - 1], "seq", -offset).astype(F32)
        key_parts.append(own[:, :HD].astype(BF16))
        value_parts.append(own[:, HD:].astype(BF16))
    key_grad = jnp.concatenate(key_parts, axis=1)
    value_grad = jnp.concatenate(value_parts, axis=1)
    return (query_grad, key_grad, value_grad, normed_grad, router_grad, routed_grads)


def solution(mesh):
    return jax.shard_map(
        on_device,
        mesh=mesh,
        in_specs=(
            P("seq", "ep"),
            P("seq", "ep"),
            P("seq", "ep"),
            P("seq", "ep"),
            P("seq"),
            P(("seq", "ep"), None),
            P(("seq", "ep"), None, None),
            P(("seq", "ep"), None),
            P(),
            P(("seq", "ep"), None),
        ),
        out_specs=(
            P("seq", "ep"),
            P("seq", "ep"),
            P("seq", "ep"),
            P(("seq", "ep"), None),
            P(),
            P(("seq", "ep"), None, None),
        ),
        check_vma=False,
    )
```

```python
import functools
import math

import jax
import jax.numpy as jnp
from jax import lax
from jax.experimental import pallas as pl
from jax.experimental.pallas import tpu as pltpu
from jax.sharding import PartitionSpec as P

EXPERTS = 8
HD = 128
TOP = 2
REACH = 3
QT = 128
MASKED = -1e30
F32 = jnp.float32
BF16 = jnp.bfloat16
VMEM_LIMIT = 48 * 1024 * 1024
SCALE = 1.0 / math.sqrt(HD)
SCALE2 = SCALE * math.log2(math.e)


def nt(a, b):
    return lax.dot_general(a, b, (((1,), (1,)), ((), ())), preferred_element_type=F32)


def nn(a, b):
    return jnp.dot(a, b, preferred_element_type=F32)


def attn_kernel(group, tok, kv_heads, start_in, seg_ref, q_ref, g_ref, k_ref, v_ref, part_ref,
                dq_ref, dk_ref, dv_ref, total_ref,
                kcat, vcat, kt, bias, dk, dv, start_ref, own, far, back, segs, one, two, two_sum, three, three_sum,
                seg_send, seg_recv, kv_send, kv_recv, far_send, far_recv,
                one_send, one_recv, two_send, two_recv, three_send, three_recv):
    window = REACH * tok + QT
    seq_size = lax.axis_size("seq")
    ep_size = lax.axis_size("ep")
    seq_me = lax.axis_index("seq")
    ep_me = lax.axis_index("ep")
    chunk = part_ref.shape[1] // ep_size

    def seq_at(by):
        return {"seq": lax.rem(seq_me + by + seq_size, seq_size)}

    def ep_at(by):
        return {"ep": lax.rem(ep_me + by, ep_size)}

    def send(src, dst, sent, landed, device):
        return pltpu.make_async_remote_copy(
            src_ref=src, dst_ref=dst, send_sem=sent, recv_sem=landed,
            device_id=device, device_id_type=pl.DeviceIdType.MESH,
        )

    barrier = pltpu.get_barrier_semaphore()
    for by in range(1, seq_size):
        pl.semaphore_signal(barrier, inc=1, device_id=seq_at(by), device_id_type=pl.DeviceIdType.MESH)
    for by in range(1, ep_size):
        pl.semaphore_signal(barrier, inc=1, device_id=ep_at(by), device_id_type=pl.DeviceIdType.MESH)
    pl.semaphore_wait(barrier, seq_size + ep_size - 2)

    seg_copies = []
    for n in range(REACH):
        seg_copies.append(send(seg_ref, segs.at[n], seg_send.at[n], seg_recv.at[n], seq_at(n + 1)))
        seg_copies[-1].start()
    kv_copies = []
    for h in range(kv_heads):
        for n in range(REACH):
            rows = pl.ds((REACH - 1 - n) * tok, tok)
            columns = pl.ds(h * HD, HD)
            for which, (src, dst) in enumerate(((k_ref, kcat), (v_ref, vcat))):
                kv_copies.append(send(
                    src.at[:, columns], dst.at[h, rows, :],
                    kv_send.at[h, n, which], kv_recv.at[h, n, which], seq_at(n + 1),
                ))
        if h == 0:
            for copy in kv_copies:
                copy.start()
            one_copies = []
            for by in range(1, ep_size):
                columns = pl.ds(pl.multiple_of(lax.rem(ep_me + by, ep_size) * chunk, 128), chunk)
                one_copies.append(send(
                    part_ref.at[:, columns], one.at[by - 1], one_send.at[by - 1], one_recv.at[by - 1], ep_at(by)
                ))
                one_copies[-1].start()
        else:
            for copy in kv_copies[-2 * REACH:]:
                copy.start()
    for h in range(kv_heads):
        kcat[h, REACH * tok:, :] = k_ref[:, h * HD:(h + 1) * HD]
        vcat[h, REACH * tok:, :] = v_ref[:, h * HD:(h + 1) * HD]

    for copy in seg_copies:
        copy.wait_recv()
    opening = seg_ref[0:1, 0:1]
    behind = jnp.zeros((1, 1), F32)
    for n in range(REACH):
        same = jnp.where(segs[n, 0:1, :] == opening, 1.0, 0.0)
        count = jnp.sum(same, axis=1, keepdims=True)
        behind += count * jnp.where(seq_me > n, 1.0, 0.0)
    shift = jnp.where(seg_ref[0:1, :] == opening, behind, 0.0)
    start_ref[...] = start_in[...] - shift.astype(jnp.int32)

    mine = pl.ds(pl.multiple_of(ep_me * chunk, 128), chunk)
    partial = part_ref[:, mine]
    for copy in one_copies:
        copy.wait_recv()
    for by in range(1, ep_size):
        partial += one[by - 1]
    two_sum[...] = partial
    two[seq_me] = partial
    two_copies = []
    for by in range(1, seq_size):
        two_copies.append(send(
            two_sum, two.at[seq_me], two_send.at[by - 1], two_recv.at[by - 1], seq_at(by)
        ))
        two_copies[-1].start()

    together = 2 if group % 2 == 0 else 1
    three_copies = []
    far_copies = []
    for h in range(kv_heads):
        for copy in kv_copies[2 * REACH * h:2 * REACH * (h + 1)]:
            copy.wait_recv()
        for n in range(REACH + 1):
            rows = slice(n * tok, (n + 1) * tok)
            kt[:, rows] = kcat[h, rows, :].astype(F32).T.astype(BF16)
        dk[...] = jnp.zeros_like(dk)
        dv[...] = jnp.zeros_like(dv)

        def rows_step(step, carry, h=h):
            base = pl.multiple_of(step * QT, QT)
            keys = pl.ds(base, window)
            rows = pl.ds(base, QT)
            position = lax.broadcasted_iota(jnp.int32, (window, QT), 0)
            limit = REACH * tok + lax.broadcasted_iota(jnp.int32, (window, QT), 1)
            allowed = (position >= start_ref[:, rows] - base) & (position <= limit)
            bias[...] = jnp.where(allowed, 0.0, MASKED)
            for first in range(h * group, (h + 1) * group, together):
                heads = range(first, first + together)
                q = jnp.concatenate([q_ref[rows, i * HD:(i + 1) * HD] for i in heads], axis=0)
                g = jnp.concatenate([g_ref[rows, i * HD:(i + 1) * HD] for i in heads], axis=0)
                scores = nt(kcat[h, keys, :], q) + jnp.concatenate([bias[...]] * together, axis=1)
                prob_grad = nt(vcat[h, keys, :], g)
                peak = jnp.max(scores, axis=0, keepdims=True)
                weights = jnp.exp2((scores - peak) * SCALE2)
                inverse = 1.0 / jnp.sum(weights, axis=0, keepdims=True)
                delta = jnp.sum(weights * prob_grad, axis=0, keepdims=True) * inverse
                probs = weights * inverse
                score_low = (probs * (prob_grad - delta)).astype(BF16)
                dv[keys, :] += nn(probs.astype(BF16), g)
                dk[keys, :] += nn(score_low, q)
                dq = (nn(kt[:, keys], score_low) * SCALE).T.astype(BF16)
                for n, i in enumerate(heads):
                    dq_ref[rows, i * HD:(i + 1) * HD] = dq[n * QT:(n + 1) * QT, :]
            return carry

        lax.fori_loop(0, tok // QT, rows_step, 0)
        for n in range(REACH):
            rows = slice((REACH - 1 - n) * tok, (REACH - n) * tok)
            far[h, n, :, :HD] = (dk[rows, :] * SCALE).astype(BF16)
            far[h, n, :, HD:] = dv[rows, :].astype(BF16)
            copy = send(far.at[h, n], back.at[h, n], far_send.at[h, n], far_recv.at[h, n], seq_at(-(n + 1)))
            copy.start()
            far_copies.append(copy)
        own[h, :, :HD] = dk[REACH * tok:, :] * SCALE
        own[h, :, HD:] = dv[REACH * tok:, :]
        if h == 0:
            for copy in two_copies:
                copy.wait_recv()
            total = two[0]
            for at in range(1, seq_size):
                total += two[at]
            three_sum[...] = total
            three[:, mine] = total
            for by in range(1, ep_size):
                three_copies.append(send(
                    three_sum, three.at[:, mine], three_send.at[by - 1], three_recv.at[by - 1], ep_at(by)
                ))
                three_copies[-1].start()

    for copy in three_copies:
        copy.wait_recv()
    total_ref[...] = three[...]
    for h in range(kv_heads):
        terms = own[h]
        for n in range(REACH):
            far_copies[h * REACH + n].wait_recv()
            terms += back[h, n].astype(F32)
        dk_ref[:, h * HD:(h + 1) * HD] = terms[:, :HD].astype(BF16)
        dv_ref[:, h * HD:(h + 1) * HD] = terms[:, HD:].astype(BF16)
    for copy in seg_copies + kv_copies + one_copies + two_copies + three_copies + far_copies:
        copy.wait_send()


def attention(start, segments, queries, attn_grad, key_heads, value_heads, part):
    tok = queries.shape[0]
    kv_heads = key_heads.shape[1] // HD
    group = queries.shape[1] // (kv_heads * HD)
    keys = (REACH + 1) * tok
    seq_size = lax.axis_size("seq")
    ep_size = lax.axis_size("ep")
    width = part.shape[1]
    chunk = width // ep_size
    work = (tok // QT) * (REACH * tok + QT) * QT * group * kv_heads
    whole = pl.BlockSpec(memory_space=pltpu.VMEM)
    dma = pltpu.SemaphoreType.DMA
    return pl.pallas_call(
        functools.partial(attn_kernel, group, tok, kv_heads),
        in_specs=[whole] * 7,
        out_specs=(whole,) * 4,
        out_shape=(
            jax.ShapeDtypeStruct(queries.shape, BF16),
            jax.ShapeDtypeStruct(key_heads.shape, BF16),
            jax.ShapeDtypeStruct(value_heads.shape, BF16),
            jax.ShapeDtypeStruct(part.shape, F32),
        ),
        scratch_shapes=[
            pltpu.VMEM((kv_heads, keys, HD), BF16),
            pltpu.VMEM((kv_heads, keys, HD), BF16),
            pltpu.VMEM((HD, keys), BF16),
            pltpu.VMEM((REACH * tok + QT, QT), F32),
            pltpu.VMEM((keys, HD), F32),
            pltpu.VMEM((keys, HD), F32),
            pltpu.VMEM((1, tok), jnp.int32),
            pltpu.VMEM((kv_heads, tok, 2 * HD), F32),
            pltpu.VMEM((kv_heads, REACH, tok, 2 * HD), BF16),
            pltpu.VMEM((kv_heads, REACH, tok, 2 * HD), BF16),
            pltpu.VMEM((REACH, 8, tok), jnp.int32),
            pltpu.VMEM((ep_size - 1, EXPERTS, chunk), F32),
            pltpu.VMEM((seq_size, EXPERTS, chunk), F32),
            pltpu.VMEM((EXPERTS, chunk), F32),
            pltpu.VMEM((EXPERTS, width), F32),
            pltpu.VMEM((EXPERTS, chunk), F32),
            dma((REACH,)),
            dma((REACH,)),
            dma((kv_heads, REACH, 2)),
            dma((kv_heads, REACH, 2)),
            dma((kv_heads, REACH)),
            dma((kv_heads, REACH)),
            dma((ep_size - 1,)),
            dma((ep_size - 1,)),
            dma((seq_size - 1,)),
            dma((seq_size - 1,)),
            dma((ep_size - 1,)),
            dma((ep_size - 1,)),
        ],
        compiler_params=pltpu.CompilerParams(
            vmem_limit_bytes=VMEM_LIMIT, collective_id=0, has_side_effects=True
        ),
        cost_estimate=pl.CostEstimate(
            flops=work * HD * 10, bytes_accessed=tok * width * 6, transcendentals=work
        ),
        name="attention",
    )(start, segments, queries, attn_grad, key_heads, value_heads, part)


def split3(x):
    high = x.astype(BF16)
    rest = x - high.astype(F32)
    mid = rest.astype(BF16)
    low = (rest - mid.astype(F32)).astype(BF16)
    return jnp.concatenate([high.astype(F32), mid.astype(F32), low.astype(F32)], axis=0).astype(BF16)


def route_kernel(capacity, copies, all_tokens, routes_ref, moe_ref, expert_ref, normed_ref, router_ref,
                 ngrad_ref, rgrad_ref, out_ref):
    rows, width = moe_ref.shape
    slots = out_ref.shape[0]
    logits = nt(router_ref[...], normed_ref[...])
    expert = lax.broadcasted_iota(jnp.int32, (EXPERTS, rows), 0)
    e0 = routes_ref[0:1, :]
    e1 = routes_ref[1:2, :]
    hot0 = (expert == e0).astype(F32)
    hot1 = (expert == e1).astype(F32)
    chosen0 = jnp.sum(hot0 * logits, axis=0, keepdims=True)
    chosen1 = jnp.sum(hot1 * logits, axis=0, keepdims=True)
    first = 1.0 / (1.0 + jnp.exp(chosen1 - chosen0))
    second = 1.0 - first
    product = nt(expert_ref[...], moe_ref[...])
    which = lax.broadcasted_iota(jnp.int32, product.shape, 0)
    token = lax.broadcasted_iota(jnp.int32, product.shape, 1)
    signed = jnp.where(which == 2 * token, product, jnp.where(which == 2 * token + 1, -product, 0.0))
    step = first * second * jnp.sum(signed, axis=0, keepdims=True)
    pieces = split3((hot0 - hot1) * step)
    earlier = lax.broadcasted_iota(jnp.int32, (rows, rows), 0) < lax.broadcasted_iota(jnp.int32, (rows, rows), 1)
    rank = nn((hot0 + hot1).astype(BF16), earlier.astype(BF16))
    rank0 = jnp.sum(hot0 * rank, axis=0, keepdims=True).astype(jnp.int32)
    rank1 = jnp.sum(hot1 * rank, axis=0, keepdims=True).astype(jnp.int32)
    slot = lax.broadcasted_iota(jnp.int32, (slots, rows), 0)
    slot = (slot // (copies * capacity)) * capacity + slot % capacity
    take0 = slot == e0 * capacity + rank0
    take1 = slot == e1 * capacity + rank1
    gate = jnp.sum(jnp.where(take0, first, 0.0) + jnp.where(take1, second, 0.0), axis=1, keepdims=True)
    pick = (take0 | take1).astype(BF16)
    chunk = 512
    for at in range(0, width, chunk):
        columns = slice(at, at + chunk)
        out_ref[:, columns] = (nn(pick, moe_ref[:, columns]) * gate).astype(BF16)
        table = jnp.concatenate([router_ref[:, columns].astype(F32)] * 3, axis=0).astype(BF16)
        ngrad_ref[:, columns] = lax.dot_general(
            pieces, table, (((0,), (0,)), ((), ())), preferred_element_type=F32
        ).astype(BF16)
        sums = nn(pieces, normed_ref[:, columns])
        rgrad_ref[:, columns] = (
            sums[0:EXPERTS] + sums[EXPERTS:2 * EXPERTS] + sums[2 * EXPERTS:]
        ) * (1.0 / all_tokens)


def on_device(queries, key_heads, value_heads, attn_grad, segments, moe_grad, expert_out, normed, router, routes):
    tok = queries.shape[0]
    ep_size = lax.axis_size("ep")
    inside = jnp.sum((segments[:, None] < segments[None, :]).astype(jnp.int32), axis=0)
    start = (REACH * tok + inside)[None, :]

    moe_rows, width = moe_grad.shape
    capacity = moe_rows * TOP // EXPERTS
    copies = max(1, ep_size // EXPERTS)
    per_device = max(1, EXPERTS // ep_size)
    slots = EXPERTS * copies * capacity
    devices = lax.axis_size("seq") * ep_size
    normed_grad, local_router, outgoing = pl.pallas_call(
        functools.partial(route_kernel, capacity, copies, moe_rows * devices),
        out_shape=(
            jax.ShapeDtypeStruct((moe_rows, width), BF16),
            jax.ShapeDtypeStruct((EXPERTS, width), F32),
            jax.ShapeDtypeStruct((slots, width), BF16),
        ),
        compiler_params=pltpu.CompilerParams(vmem_limit_bytes=VMEM_LIMIT),
        cost_estimate=pl.CostEstimate(flops=8 * slots * moe_rows * width, bytes_accessed=12 * moe_rows * width, transcendentals=0),
        name="routing",
    )(routes.T, moe_grad, expert_out.reshape(TOP * moe_rows, width), normed, router)
    routed_grads = lax.all_to_all(
        outgoing.reshape(ep_size, per_device * capacity, width), "ep", split_axis=0, concat_axis=0, tiled=True
    )
    query_grad, key_grad, value_grad, router_grad = attention(
        start, jnp.broadcast_to(segments[None, :], (8, tok)), queries, attn_grad, key_heads, value_heads, local_router
    )
    return (query_grad, key_grad, value_grad, normed_grad, router_grad, routed_grads)


def solution(mesh):
    return jax.shard_map(
        on_device,
        mesh=mesh,
        in_specs=(
            P("seq", "ep"),
            P("seq", "ep"),
            P("seq", "ep"),
            P("seq", "ep"),
            P("seq"),
            P(("seq", "ep"), None),
            P(("seq", "ep"), None, None),
            P(("seq", "ep"), None),
            P(),
            P(("seq", "ep"), None),
        ),
        out_specs=(
            P("seq", "ep"),
            P("seq", "ep"),
            P("seq", "ep"),
            P(("seq", "ep"), None),
            P(),
            P(("seq", "ep"), None, None),
        ),
        check_vma=False,
    )
```

```python
import functools
import math

import jax
import jax.numpy as jnp
from jax import lax
from jax.experimental import pallas as pl
from jax.experimental.pallas import tpu as pltpu
from jax.sharding import PartitionSpec as P

EXPERTS = 8
HD = 128
TOP = 2
REACH = 3
QT = 128
MASKED = -1e30
F32 = jnp.float32
BF16 = jnp.bfloat16
VMEM_LIMIT = 48 * 1024 * 1024
SCALE = 1.0 / math.sqrt(HD)
SCALE2 = SCALE * math.log2(math.e)


def nt(a, b):
    return lax.dot_general(a, b, (((1,), (1,)), ((), ())), preferred_element_type=F32)


def nn(a, b):
    return jnp.dot(a, b, preferred_element_type=F32)


def attn_kernel(group, tok, kv_heads, start_in, seg_ref, q_ref, g_ref, k_ref, v_ref, part_ref,
                dq_ref, dk_ref, dv_ref, total_ref,
                kcat, vcat, kt, bias, dk, dv, start_ref, own, far, back, segs, one, two, two_sum, three, three_sum,
                seg_send, seg_recv, kv_send, kv_recv, far_send, far_recv,
                one_send, one_recv, two_send, two_recv, three_send, three_recv):
    window = REACH * tok + QT
    seq_size = lax.axis_size("seq")
    ep_size = lax.axis_size("ep")
    seq_me = lax.axis_index("seq")
    ep_me = lax.axis_index("ep")
    chunk = part_ref.shape[1] // ep_size

    def seq_at(by):
        return {"seq": lax.rem(seq_me + by + seq_size, seq_size)}

    def ep_at(by):
        return {"ep": lax.rem(ep_me + by, ep_size)}

    def send(src, dst, sent, landed, device):
        return pltpu.make_async_remote_copy(
            src_ref=src, dst_ref=dst, send_sem=sent, recv_sem=landed,
            device_id=device, device_id_type=pl.DeviceIdType.MESH,
        )

    barrier = pltpu.get_barrier_semaphore()
    for by in range(1, seq_size):
        pl.semaphore_signal(barrier, inc=1, device_id=seq_at(by), device_id_type=pl.DeviceIdType.MESH)
    for by in range(1, ep_size):
        pl.semaphore_signal(barrier, inc=1, device_id=ep_at(by), device_id_type=pl.DeviceIdType.MESH)
    pl.semaphore_wait(barrier, seq_size + ep_size - 2)

    seg_copies = []
    for n in range(REACH):
        seg_copies.append(send(seg_ref, segs.at[n], seg_send.at[n], seg_recv.at[n], seq_at(n + 1)))
        seg_copies[-1].start()
    odd = lax.rem(seq_me, 2)
    even_here = odd == 0
    odd_here = odd == 1

    def kv(h, kind):
        columns = pl.ds(h * HD, HD)
        second = pl.ds(tok, tok)
        third = pl.ds(2 * tok, tok)
        copies = []
        for which, (source, buffer) in enumerate(((k_ref, kcat), (v_ref, vcat))):
            if kind == 0:
                src, rows, device = source.at[:, columns], second, seq_at(2)
            elif kind == 1:
                rows = pl.ds(pl.multiple_of(2 * odd * tok, QT), tok)
                src, device = buffer.at[h, second, :], seq_at(1 - 2 * odd)
            elif kind == 2:
                src, rows, device = source.at[:, columns], third, seq_at(1)
            else:
                src, rows, device = buffer.at[h, third, :], pl.ds(0, tok), seq_at(2)
            copies.append(send(
                src, buffer.at[h, rows, :], kv_send.at[h, kind, which], kv_recv.at[h, kind, which], device
            ))
        return copies

    def begin(copies):
        for copy in copies:
            copy.start()

    def landed(copies):
        for copy in copies:
            copy.wait_recv()

    def pass_pair(h):
        landed(kv(h, 0))
        begin(kv(h, 1))

    def pass_on(h):
        @pl.when(even_here)
        def _():
            landed(kv(h, 1))
            begin(kv(h, 3))

    def keys_here(h):
        @pl.when(even_here)
        def _():
            landed(kv(h, 3))

        @pl.when(odd_here)
        def _():
            landed(kv(h, 1))
            landed(kv(h, 2))

    def term(h, kind):
        source = (2, 2, 0, 0, 1)[kind]
        device = seq_at((-2, -1, -1, 1, -2)[kind])
        return send(far.at[h, source], back.at[h, kind], far_send.at[h, kind], far_recv.at[h, kind], device)

    def add_to(h, source, kind):
        term(h, kind).wait_recv()
        far[h, source] = (far[h, source].astype(F32) + back[h, kind].astype(F32)).astype(BF16)

    def terms_out(h):
        @pl.when(even_here)
        def _():
            term(h, 0).start()

        @pl.when(odd_here)
        def _():
            term(h, 1).start()
            term(h, 2).start()

    def terms_even(h):
        @pl.when(even_here)
        def _():
            add_to(h, 0, 0)
            term(h, 3).start()
            add_to(h, 1, 1)
            term(h, 4).start()

    def terms_odd(h):
        @pl.when(odd_here)
        def _():
            add_to(h, 1, 3)
            term(h, 4).start()

    def terms_in(h):
        @pl.when(even_here)
        def _():
            term(h, 2).wait_recv()
            own[h] += back[h, 2].astype(F32)

        term(h, 4).wait_recv()
        terms = own[h] + back[h, 4].astype(F32)
        dk_ref[:, h * HD:(h + 1) * HD] = terms[:, :HD].astype(BF16)
        dv_ref[:, h * HD:(h + 1) * HD] = terms[:, HD:].astype(BF16)

    one_copies = []
    for h in range(kv_heads):
        begin(kv(h, 0))

        @pl.when(even_here)
        def _(h=h):
            begin(kv(h, 2))

        if h == 0:
            for by in range(1, ep_size):
                columns = pl.ds(pl.multiple_of(lax.rem(ep_me + by, ep_size) * chunk, 128), chunk)
                one_copies.append(send(
                    part_ref.at[:, columns], one.at[by - 1], one_send.at[by - 1], one_recv.at[by - 1], ep_at(by)
                ))
            begin(one_copies)
    for h in range(kv_heads):
        kcat[h, REACH * tok:, :] = k_ref[:, h * HD:(h + 1) * HD]
        vcat[h, REACH * tok:, :] = v_ref[:, h * HD:(h + 1) * HD]

    for copy in seg_copies:
        copy.wait_recv()
    opening = seg_ref[0:1, 0:1]
    behind = jnp.zeros((1, 1), F32)
    for n in range(REACH):
        same = jnp.where(segs[n, 0:1, :] == opening, 1.0, 0.0)
        count = jnp.sum(same, axis=1, keepdims=True)
        behind += count * jnp.where(seq_me > n, 1.0, 0.0)
    shift = jnp.where(seg_ref[0:1, :] == opening, behind, 0.0)
    start_ref[...] = start_in[...] - shift.astype(jnp.int32)

    mine = pl.ds(pl.multiple_of(ep_me * chunk, 128), chunk)
    partial = part_ref[:, mine]
    for copy in one_copies:
        copy.wait_recv()
    for by in range(1, ep_size):
        partial += one[by - 1]
    two_sum[...] = partial
    two[seq_me] = partial
    two_copies = []
    for by in range(1, seq_size):
        two_copies.append(send(
            two_sum, two.at[seq_me], two_send.at[by - 1], two_recv.at[by - 1], seq_at(by)
        ))
        two_copies[-1].start()

    together = 2 if group % 2 == 0 else 1
    three_copies = []
    pass_pair(0)
    pass_on(0)
    for h in range(1, kv_heads):
        pass_pair(h)
    for h in range(kv_heads):
        keys_here(h)
        for n in range(REACH + 1):
            rows = slice(n * tok, (n + 1) * tok)
            kt[:, rows] = kcat[h, rows, :].astype(F32).T.astype(BF16)
        dk[...] = jnp.zeros_like(dk)
        dv[...] = jnp.zeros_like(dv)

        def rows_step(step, carry, h=h):
            base = pl.multiple_of(step * QT, QT)
            keys = pl.ds(base, window)
            rows = pl.ds(base, QT)
            position = lax.broadcasted_iota(jnp.int32, (window, QT), 0)
            limit = REACH * tok + lax.broadcasted_iota(jnp.int32, (window, QT), 1)
            allowed = (position >= start_ref[:, rows] - base) & (position <= limit)
            bias[...] = jnp.where(allowed, 0.0, MASKED)
            for first in range(h * group, (h + 1) * group, together):
                heads = range(first, first + together)
                q = jnp.concatenate([q_ref[rows, i * HD:(i + 1) * HD] for i in heads], axis=0)
                g = jnp.concatenate([g_ref[rows, i * HD:(i + 1) * HD] for i in heads], axis=0)
                scores = nt(kcat[h, keys, :], q) + jnp.concatenate([bias[...]] * together, axis=1)
                prob_grad = nt(vcat[h, keys, :], g)
                peak = jnp.max(scores, axis=0, keepdims=True)
                weights = jnp.exp2((scores - peak) * SCALE2)
                inverse = 1.0 / jnp.sum(weights, axis=0, keepdims=True)
                delta = jnp.sum(weights * prob_grad, axis=0, keepdims=True) * inverse
                probs = weights * inverse
                score_low = (probs * (prob_grad - delta)).astype(BF16)
                dv[keys, :] += nn(probs.astype(BF16), g)
                dk[keys, :] += nn(score_low, q)
                dq = (nn(kt[:, keys], score_low) * SCALE).T.astype(BF16)
                for n, i in enumerate(heads):
                    dq_ref[rows, i * HD:(i + 1) * HD] = dq[n * QT:(n + 1) * QT, :]

            @pl.when(step == 0)
            def _():
                if h + 1 < kv_heads:
                    pass_on(h + 1)
                if h > 0:
                    terms_even(h - 1)

            if h > 0:
                @pl.when(step == 1)
                def _():
                    terms_odd(h - 1)

            return carry

        lax.fori_loop(0, tok // QT, rows_step, 0)
        for n in range(REACH):
            rows = slice((REACH - 1 - n) * tok, (REACH - n) * tok)
            far[h, n, :, :HD] = (dk[rows, :] * SCALE).astype(BF16)
            far[h, n, :, HD:] = dv[rows, :].astype(BF16)
        terms_out(h)
        own[h, :, :HD] = dk[REACH * tok:, :] * SCALE
        own[h, :, HD:] = dv[REACH * tok:, :]
        if h == 0:
            for copy in two_copies:
                copy.wait_recv()
            total = two[0]
            for at in range(1, seq_size):
                total += two[at]
            three_sum[...] = total
            three[:, mine] = total
            for by in range(1, ep_size):
                three_copies.append(send(
                    three_sum, three.at[:, mine], three_send.at[by - 1], three_recv.at[by - 1], ep_at(by)
                ))
                three_copies[-1].start()

    for h in range(kv_heads - 1):
        terms_in(h)
    terms_even(kv_heads - 1)
    landed(three_copies)
    total_ref[...] = three[...]
    terms_odd(kv_heads - 1)
    terms_in(kv_heads - 1)

    for copy in seg_copies + one_copies + two_copies + three_copies:
        copy.wait_send()
    for h in range(kv_heads):
        for copy in kv(h, 0) + kv(h, 1) + [term(h, 4)]:
            copy.wait_send()

        @pl.when(even_here)
        def _(h=h):
            for copy in kv(h, 2) + kv(h, 3) + [term(h, 0), term(h, 3)]:
                copy.wait_send()

        @pl.when(odd_here)
        def _(h=h):
            term(h, 1).wait_send()
            term(h, 2).wait_send()


def attention(start, segments, queries, attn_grad, key_heads, value_heads, part):
    tok = queries.shape[0]
    kv_heads = key_heads.shape[1] // HD
    group = queries.shape[1] // (kv_heads * HD)
    keys = (REACH + 1) * tok
    seq_size = lax.axis_size("seq")
    ep_size = lax.axis_size("ep")
    width = part.shape[1]
    chunk = width // ep_size
    work = (tok // QT) * (REACH * tok + QT) * QT * group * kv_heads
    whole = pl.BlockSpec(memory_space=pltpu.VMEM)
    dma = pltpu.SemaphoreType.DMA
    return pl.pallas_call(
        functools.partial(attn_kernel, group, tok, kv_heads),
        in_specs=[whole] * 7,
        out_specs=(whole,) * 4,
        out_shape=(
            jax.ShapeDtypeStruct(queries.shape, BF16),
            jax.ShapeDtypeStruct(key_heads.shape, BF16),
            jax.ShapeDtypeStruct(value_heads.shape, BF16),
            jax.ShapeDtypeStruct(part.shape, F32),
        ),
        scratch_shapes=[
            pltpu.VMEM((kv_heads, keys, HD), BF16),
            pltpu.VMEM((kv_heads, keys, HD), BF16),
            pltpu.VMEM((HD, keys), BF16),
            pltpu.VMEM((REACH * tok + QT, QT), F32),
            pltpu.VMEM((keys, HD), F32),
            pltpu.VMEM((keys, HD), F32),
            pltpu.VMEM((1, tok), jnp.int32),
            pltpu.VMEM((kv_heads, tok, 2 * HD), F32),
            pltpu.VMEM((kv_heads, REACH, tok, 2 * HD), BF16),
            pltpu.VMEM((kv_heads, 5, tok, 2 * HD), BF16),
            pltpu.VMEM((REACH, 8, tok), jnp.int32),
            pltpu.VMEM((ep_size - 1, EXPERTS, chunk), F32),
            pltpu.VMEM((seq_size, EXPERTS, chunk), F32),
            pltpu.VMEM((EXPERTS, chunk), F32),
            pltpu.VMEM((EXPERTS, width), F32),
            pltpu.VMEM((EXPERTS, chunk), F32),
            dma((REACH,)),
            dma((REACH,)),
            dma((kv_heads, 4, 2)),
            dma((kv_heads, 4, 2)),
            dma((kv_heads, 5)),
            dma((kv_heads, 5)),
            dma((ep_size - 1,)),
            dma((ep_size - 1,)),
            dma((seq_size - 1,)),
            dma((seq_size - 1,)),
            dma((ep_size - 1,)),
            dma((ep_size - 1,)),
        ],
        compiler_params=pltpu.CompilerParams(
            vmem_limit_bytes=VMEM_LIMIT, collective_id=0, has_side_effects=True
        ),
        cost_estimate=pl.CostEstimate(
            flops=work * HD * 10, bytes_accessed=tok * width * 6, transcendentals=work
        ),
        name="attention",
    )(start, segments, queries, attn_grad, key_heads, value_heads, part)


def split3(x):
    high = x.astype(BF16)
    rest = x - high.astype(F32)
    mid = rest.astype(BF16)
    low = (rest - mid.astype(F32)).astype(BF16)
    return jnp.concatenate([high.astype(F32), mid.astype(F32), low.astype(F32)], axis=0).astype(BF16)


def route_kernel(capacity, copies, all_tokens, routes_ref, moe_ref, expert_ref, normed_ref, router_ref,
                 ngrad_ref, rgrad_ref, out_ref):
    rows, width = moe_ref.shape
    slots = out_ref.shape[0]
    logits = nt(router_ref[...], normed_ref[...])
    expert = lax.broadcasted_iota(jnp.int32, (EXPERTS, rows), 0)
    e0 = routes_ref[0:1, :]
    e1 = routes_ref[1:2, :]
    hot0 = (expert == e0).astype(F32)
    hot1 = (expert == e1).astype(F32)
    chosen0 = jnp.sum(hot0 * logits, axis=0, keepdims=True)
    chosen1 = jnp.sum(hot1 * logits, axis=0, keepdims=True)
    first = 1.0 / (1.0 + jnp.exp(chosen1 - chosen0))
    second = 1.0 - first
    product = nt(expert_ref[...], moe_ref[...])
    which = lax.broadcasted_iota(jnp.int32, product.shape, 0)
    token = lax.broadcasted_iota(jnp.int32, product.shape, 1)
    signed = jnp.where(which == 2 * token, product, jnp.where(which == 2 * token + 1, -product, 0.0))
    step = first * second * jnp.sum(signed, axis=0, keepdims=True)
    pieces = split3((hot0 - hot1) * step)
    earlier = lax.broadcasted_iota(jnp.int32, (rows, rows), 0) < lax.broadcasted_iota(jnp.int32, (rows, rows), 1)
    rank = nn((hot0 + hot1).astype(BF16), earlier.astype(BF16))
    rank0 = jnp.sum(hot0 * rank, axis=0, keepdims=True).astype(jnp.int32)
    rank1 = jnp.sum(hot1 * rank, axis=0, keepdims=True).astype(jnp.int32)
    slot = lax.broadcasted_iota(jnp.int32, (slots, rows), 0)
    slot = (slot // (copies * capacity)) * capacity + slot % capacity
    take0 = slot == e0 * capacity + rank0
    take1 = slot == e1 * capacity + rank1
    gate = jnp.sum(jnp.where(take0, first, 0.0) + jnp.where(take1, second, 0.0), axis=1, keepdims=True)
    pick = (take0 | take1).astype(BF16)
    chunk = 512
    for at in range(0, width, chunk):
        columns = slice(at, at + chunk)
        out_ref[:, columns] = (nn(pick, moe_ref[:, columns]) * gate).astype(BF16)
        table = jnp.concatenate([router_ref[:, columns].astype(F32)] * 3, axis=0).astype(BF16)
        ngrad_ref[:, columns] = lax.dot_general(
            pieces, table, (((0,), (0,)), ((), ())), preferred_element_type=F32
        ).astype(BF16)
        sums = nn(pieces, normed_ref[:, columns])
        rgrad_ref[:, columns] = (
            sums[0:EXPERTS] + sums[EXPERTS:2 * EXPERTS] + sums[2 * EXPERTS:]
        ) * (1.0 / all_tokens)


def on_device(queries, key_heads, value_heads, attn_grad, segments, moe_grad, expert_out, normed, router, routes):
    tok = queries.shape[0]
    ep_size = lax.axis_size("ep")
    inside = jnp.sum((segments[:, None] < segments[None, :]).astype(jnp.int32), axis=0)
    start = (REACH * tok + inside)[None, :]

    moe_rows, width = moe_grad.shape
    capacity = moe_rows * TOP // EXPERTS
    copies = max(1, ep_size // EXPERTS)
    per_device = max(1, EXPERTS // ep_size)
    slots = EXPERTS * copies * capacity
    devices = lax.axis_size("seq") * ep_size
    normed_grad, local_router, outgoing = pl.pallas_call(
        functools.partial(route_kernel, capacity, copies, moe_rows * devices),
        out_shape=(
            jax.ShapeDtypeStruct((moe_rows, width), BF16),
            jax.ShapeDtypeStruct((EXPERTS, width), F32),
            jax.ShapeDtypeStruct((slots, width), BF16),
        ),
        compiler_params=pltpu.CompilerParams(vmem_limit_bytes=VMEM_LIMIT),
        cost_estimate=pl.CostEstimate(flops=8 * slots * moe_rows * width, bytes_accessed=12 * moe_rows * width, transcendentals=0),
        name="routing",
    )(routes.T, moe_grad, expert_out.reshape(TOP * moe_rows, width), normed, router)
    routed_grads = lax.all_to_all(
        outgoing.reshape(ep_size, per_device * capacity, width), "ep", split_axis=0, concat_axis=0, tiled=True
    )
    query_grad, key_grad, value_grad, router_grad = attention(
        start, jnp.broadcast_to(segments[None, :], (8, tok)), queries, attn_grad, key_heads, value_heads, local_router
    )
    return (query_grad, key_grad, value_grad, normed_grad, router_grad, routed_grads)


def solution(mesh):
    return jax.shard_map(
        on_device,
        mesh=mesh,
        in_specs=(
            P("seq", "ep"),
            P("seq", "ep"),
            P("seq", "ep"),
            P("seq", "ep"),
            P("seq"),
            P(("seq", "ep"), None),
            P(("seq", "ep"), None, None),
            P(("seq", "ep"), None),
            P(),
            P(("seq", "ep"), None),
        ),
        out_specs=(
            P("seq", "ep"),
            P("seq", "ep"),
            P("seq", "ep"),
            P(("seq", "ep"), None),
            P(),
            P(("seq", "ep"), None, None),
        ),
        check_vma=False,
    )
```

```python
import functools
import math

import jax
import jax.numpy as jnp
from jax import lax
from jax.experimental import pallas as pl
from jax.experimental.pallas import tpu as pltpu
from jax.sharding import PartitionSpec as P

EXPERTS = 8
HD = 128
TOP = 2
REACH = 3
QT = 128
MASKED = -1e30
F32 = jnp.float32
BF16 = jnp.bfloat16
VMEM_LIMIT = 48 * 1024 * 1024
SCALE = 1.0 / math.sqrt(HD)
SCALE2 = SCALE * math.log2(math.e)


def nt(a, b):
    return lax.dot_general(a, b, (((1,), (1,)), ((), ())), preferred_element_type=F32)


def nn(a, b):
    return jnp.dot(a, b, preferred_element_type=F32)


def attn_kernel(group, tok, kv_heads, start_in, seg_ref, q_ref, g_ref, k_ref, v_ref, part_ref,
                dq_ref, dk_ref, dv_ref, total_ref,
                kcat, vcat, kt, bias, dk, dv, start_ref, own, far, back, segs, one, two, two_sum, three, three_sum,
                seg_send, seg_recv, kv_send, kv_recv, far_send, far_recv,
                one_send, one_recv, two_send, two_recv, three_send, three_recv):
    window = REACH * tok + QT
    seq_size = lax.axis_size("seq")
    ep_size = lax.axis_size("ep")
    seq_me = lax.axis_index("seq")
    ep_me = lax.axis_index("ep")
    chunk = part_ref.shape[1] // ep_size

    def seq_at(by):
        return {"seq": lax.rem(seq_me + by + seq_size, seq_size)}

    def ep_at(by):
        return {"ep": lax.rem(ep_me + by, ep_size)}

    def send(src, dst, sent, landed, device):
        return pltpu.make_async_remote_copy(
            src_ref=src, dst_ref=dst, send_sem=sent, recv_sem=landed,
            device_id=device, device_id_type=pl.DeviceIdType.MESH,
        )

    barrier = pltpu.get_barrier_semaphore()
    for by in range(1, seq_size):
        pl.semaphore_signal(barrier, inc=1, device_id=seq_at(by), device_id_type=pl.DeviceIdType.MESH)
    for by in range(1, ep_size):
        pl.semaphore_signal(barrier, inc=1, device_id=ep_at(by), device_id_type=pl.DeviceIdType.MESH)
    pl.semaphore_wait(barrier, seq_size + ep_size - 2)

    seg_copies = []
    for n in range(REACH):
        seg_copies.append(send(seg_ref, segs.at[n], seg_send.at[n], seg_recv.at[n], seq_at(n + 1)))
        seg_copies[-1].start()
    odd = lax.rem(seq_me, 2)
    even_here = odd == 0
    odd_here = odd == 1

    def kv(h, kind):
        columns = pl.ds(h * HD, HD)
        second = pl.ds(tok, tok)
        third = pl.ds(2 * tok, tok)
        copies = []
        for which, (source, buffer) in enumerate(((k_ref, kcat), (v_ref, vcat))):
            if kind == 0:
                src, rows, device = source.at[:, columns], second, seq_at(2)
            elif kind == 1:
                rows = pl.ds(pl.multiple_of(2 * odd * tok, QT), tok)
                src, device = buffer.at[h, second, :], seq_at(1 - 2 * odd)
            elif kind == 2:
                src, rows, device = source.at[:, columns], third, seq_at(1)
            else:
                src, rows, device = buffer.at[h, third, :], pl.ds(0, tok), seq_at(2)
            copies.append(send(
                src, buffer.at[h, rows, :], kv_send.at[h, kind, which], kv_recv.at[h, kind, which], device
            ))
        return copies

    def begin(copies):
        for copy in copies:
            copy.start()

    def landed(copies):
        for copy in copies:
            copy.wait_recv()

    def pass_pair(h):
        landed(kv(h, 0))
        begin(kv(h, 1))

    def pass_on(h):
        @pl.when(even_here)
        def _():
            landed(kv(h, 1))
            begin(kv(h, 3))

    def keys_here(h):
        @pl.when(even_here)
        def _():
            landed(kv(h, 3))

        @pl.when(odd_here)
        def _():
            landed(kv(h, 1))
            landed(kv(h, 2))

    def term(h, kind):
        source = (2, 2, 0, 0, 1)[kind]
        device = seq_at((-2, -1, -1, 1, -2)[kind])
        return send(far.at[h, source], back.at[h, kind], far_send.at[h, kind], far_recv.at[h, kind], device)

    def add_to(h, source, kind):
        term(h, kind).wait_recv()
        far[h, source] = (far[h, source].astype(F32) + back[h, kind].astype(F32)).astype(BF16)

    def terms_out(h):
        @pl.when(even_here)
        def _():
            term(h, 0).start()

        @pl.when(odd_here)
        def _():
            term(h, 1).start()
            term(h, 2).start()

    def terms_even(h):
        @pl.when(even_here)
        def _():
            add_to(h, 0, 0)
            term(h, 3).start()
            add_to(h, 1, 1)
            term(h, 4).start()

    def terms_odd(h):
        @pl.when(odd_here)
        def _():
            add_to(h, 1, 3)
            term(h, 4).start()

    def terms_in(h):
        @pl.when(even_here)
        def _():
            term(h, 2).wait_recv()
            own[h] += back[h, 2].astype(F32)

        term(h, 4).wait_recv()
        terms = own[h] + back[h, 4].astype(F32)
        dk_ref[:, h * HD:(h + 1) * HD] = terms[:, :HD].astype(BF16)
        dv_ref[:, h * HD:(h + 1) * HD] = terms[:, HD:].astype(BF16)

    one_copies = []
    for h in range(kv_heads):
        begin(kv(h, 0))

        @pl.when(even_here)
        def _(h=h):
            begin(kv(h, 2))

        if h == 0:
            for by in range(1, ep_size):
                columns = pl.ds(pl.multiple_of(lax.rem(ep_me + by, ep_size) * chunk, 128), chunk)
                one_copies.append(send(
                    part_ref.at[:, columns], one.at[by - 1], one_send.at[by - 1], one_recv.at[by - 1], ep_at(by)
                ))
            begin(one_copies)
    for h in range(kv_heads):
        kcat[h, REACH * tok:, :] = k_ref[:, h * HD:(h + 1) * HD]
        vcat[h, REACH * tok:, :] = v_ref[:, h * HD:(h + 1) * HD]

    for copy in seg_copies:
        copy.wait_recv()
    opening = seg_ref[0:1, 0:1]
    behind = jnp.zeros((1, 1), F32)
    for n in range(REACH):
        same = jnp.where(segs[n, 0:1, :] == opening, 1.0, 0.0)
        count = jnp.sum(same, axis=1, keepdims=True)
        behind += count * jnp.where(seq_me > n, 1.0, 0.0)
    shift = jnp.where(seg_ref[0:1, :] == opening, behind, 0.0)
    start_ref[...] = start_in[...] - shift.astype(jnp.int32)

    mine = pl.ds(pl.multiple_of(ep_me * chunk, 128), chunk)
    together = 2 if group % 2 == 0 else 1
    three_copies = []
    pass_pair(0)
    pass_on(0)
    for h in range(1, kv_heads):
        pass_pair(h)
    for h in range(kv_heads):
        keys_here(h)
        for n in range(REACH + 1):
            rows = slice(n * tok, (n + 1) * tok)
            kt[:, rows] = kcat[h, rows, :].astype(F32).T.astype(BF16)
        dk[...] = jnp.zeros_like(dk)
        dv[...] = jnp.zeros_like(dv)

        def rows_step(step, carry, h=h):
            base = pl.multiple_of(step * QT, QT)
            keys = pl.ds(base, window)
            rows = pl.ds(base, QT)
            position = lax.broadcasted_iota(jnp.int32, (window, QT), 0)
            limit = REACH * tok + lax.broadcasted_iota(jnp.int32, (window, QT), 1)
            allowed = (position >= start_ref[:, rows] - base) & (position <= limit)
            bias[...] = jnp.where(allowed, 0.0, MASKED)
            for first in range(h * group, (h + 1) * group, together):
                heads = range(first, first + together)
                q = jnp.concatenate([q_ref[rows, i * HD:(i + 1) * HD] for i in heads], axis=0)
                g = jnp.concatenate([g_ref[rows, i * HD:(i + 1) * HD] for i in heads], axis=0)
                scores = nt(kcat[h, keys, :], q) + jnp.concatenate([bias[...]] * together, axis=1)
                prob_grad = nt(vcat[h, keys, :], g)
                peak = jnp.max(scores, axis=0, keepdims=True)
                weights = jnp.exp2((scores - peak) * SCALE2)
                inverse = 1.0 / jnp.sum(weights, axis=0, keepdims=True)
                delta = jnp.sum(weights * prob_grad, axis=0, keepdims=True) * inverse
                probs = weights * inverse
                score_low = (probs * (prob_grad - delta)).astype(BF16)
                dv[keys, :] += nn(probs.astype(BF16), g)
                dk[keys, :] += nn(score_low, q)
                dq = (nn(kt[:, keys], score_low) * SCALE).T.astype(BF16)
                for n, i in enumerate(heads):
                    dq_ref[rows, i * HD:(i + 1) * HD] = dq[n * QT:(n + 1) * QT, :]

            @pl.when(step == 0)
            def _():
                if h + 1 < kv_heads:
                    pass_on(h + 1)
                if h > 0:
                    terms_even(h - 1)

            if h > 0:
                @pl.when(step == 1)
                def _():
                    terms_odd(h - 1)

            return carry

        lax.fori_loop(0, tok // QT, rows_step, 0)
        for n in range(REACH):
            rows = slice((REACH - 1 - n) * tok, (REACH - n) * tok)
            far[h, n, :, :HD] = (dk[rows, :] * SCALE).astype(BF16)
            far[h, n, :, HD:] = dv[rows, :].astype(BF16)
        terms_out(h)
        own[h, :, :HD] = dk[REACH * tok:, :] * SCALE
        own[h, :, HD:] = dv[REACH * tok:, :]
        if h == 0:
            partial = part_ref[:, mine]
            for copy in one_copies:
                copy.wait_recv()
            for by in range(1, ep_size):
                partial += one[by - 1]
            two_sum[...] = partial
            two[seq_me] = partial
            two_copies = []
            for by in range(1, seq_size):
                two_copies.append(send(
                    two_sum, two.at[seq_me], two_send.at[by - 1], two_recv.at[by - 1], seq_at(by)
                ))
                two_copies[-1].start()

    for copy in two_copies:
        copy.wait_recv()
    total = two[0]
    for at in range(1, seq_size):
        total += two[at]
    three_sum[...] = total
    three[:, mine] = total
    for by in range(1, ep_size):
        three_copies.append(send(
            three_sum, three.at[:, mine], three_send.at[by - 1], three_recv.at[by - 1], ep_at(by)
        ))
        three_copies[-1].start()
    for h in range(kv_heads - 1):
        terms_in(h)
    terms_even(kv_heads - 1)
    terms_odd(kv_heads - 1)
    landed(three_copies)
    total_ref[...] = three[...]
    terms_in(kv_heads - 1)

    for copy in seg_copies + one_copies + two_copies + three_copies:
        copy.wait_send()
    for h in range(kv_heads):
        for copy in kv(h, 0) + kv(h, 1) + [term(h, 4)]:
            copy.wait_send()

        @pl.when(even_here)
        def _(h=h):
            for copy in kv(h, 2) + kv(h, 3) + [term(h, 0), term(h, 3)]:
                copy.wait_send()

        @pl.when(odd_here)
        def _(h=h):
            term(h, 1).wait_send()
            term(h, 2).wait_send()


def attention(start, segments, queries, attn_grad, key_heads, value_heads, part):
    tok = queries.shape[0]
    kv_heads = key_heads.shape[1] // HD
    group = queries.shape[1] // (kv_heads * HD)
    keys = (REACH + 1) * tok
    seq_size = lax.axis_size("seq")
    ep_size = lax.axis_size("ep")
    width = part.shape[1]
    chunk = width // ep_size
    work = (tok // QT) * (REACH * tok + QT) * QT * group * kv_heads
    whole = pl.BlockSpec(memory_space=pltpu.VMEM)
    dma = pltpu.SemaphoreType.DMA
    return pl.pallas_call(
        functools.partial(attn_kernel, group, tok, kv_heads),
        in_specs=[whole] * 7,
        out_specs=(whole,) * 4,
        out_shape=(
            jax.ShapeDtypeStruct(queries.shape, BF16),
            jax.ShapeDtypeStruct(key_heads.shape, BF16),
            jax.ShapeDtypeStruct(value_heads.shape, BF16),
            jax.ShapeDtypeStruct(part.shape, F32),
        ),
        scratch_shapes=[
            pltpu.VMEM((kv_heads, keys, HD), BF16),
            pltpu.VMEM((kv_heads, keys, HD), BF16),
            pltpu.VMEM((HD, keys), BF16),
            pltpu.VMEM((REACH * tok + QT, QT), F32),
            pltpu.VMEM((keys, HD), F32),
            pltpu.VMEM((keys, HD), F32),
            pltpu.VMEM((1, tok), jnp.int32),
            pltpu.VMEM((kv_heads, tok, 2 * HD), F32),
            pltpu.VMEM((kv_heads, REACH, tok, 2 * HD), BF16),
            pltpu.VMEM((kv_heads, 5, tok, 2 * HD), BF16),
            pltpu.VMEM((REACH, 8, tok), jnp.int32),
            pltpu.VMEM((ep_size - 1, EXPERTS, chunk), F32),
            pltpu.VMEM((seq_size, EXPERTS, chunk), F32),
            pltpu.VMEM((EXPERTS, chunk), F32),
            pltpu.VMEM((EXPERTS, width), F32),
            pltpu.VMEM((EXPERTS, chunk), F32),
            dma((REACH,)),
            dma((REACH,)),
            dma((kv_heads, 4, 2)),
            dma((kv_heads, 4, 2)),
            dma((kv_heads, 5)),
            dma((kv_heads, 5)),
            dma((ep_size - 1,)),
            dma((ep_size - 1,)),
            dma((seq_size - 1,)),
            dma((seq_size - 1,)),
            dma((ep_size - 1,)),
            dma((ep_size - 1,)),
        ],
        compiler_params=pltpu.CompilerParams(
            vmem_limit_bytes=VMEM_LIMIT, collective_id=0, has_side_effects=True
        ),
        cost_estimate=pl.CostEstimate(
            flops=work * HD * 10, bytes_accessed=tok * width * 6, transcendentals=work
        ),
        name="attention",
    )(start, segments, queries, attn_grad, key_heads, value_heads, part)


def split3(x):
    high = x.astype(BF16)
    rest = x - high.astype(F32)
    mid = rest.astype(BF16)
    low = (rest - mid.astype(F32)).astype(BF16)
    return jnp.concatenate([high.astype(F32), mid.astype(F32), low.astype(F32)], axis=0).astype(BF16)


def route_kernel(capacity, copies, all_tokens, routes_ref, moe_ref, expert_ref, normed_ref, router_ref,
                 ngrad_ref, rgrad_ref, out_ref):
    rows, width = moe_ref.shape
    slots = out_ref.shape[0]
    logits = nt(router_ref[...], normed_ref[...])
    expert = lax.broadcasted_iota(jnp.int32, (EXPERTS, rows), 0)
    e0 = routes_ref[0:1, :]
    e1 = routes_ref[1:2, :]
    hot0 = (expert == e0).astype(F32)
    hot1 = (expert == e1).astype(F32)
    chosen0 = jnp.sum(hot0 * logits, axis=0, keepdims=True)
    chosen1 = jnp.sum(hot1 * logits, axis=0, keepdims=True)
    first = 1.0 / (1.0 + jnp.exp(chosen1 - chosen0))
    second = 1.0 - first
    product = nt(expert_ref[...], moe_ref[...])
    which = lax.broadcasted_iota(jnp.int32, product.shape, 0)
    token = lax.broadcasted_iota(jnp.int32, product.shape, 1)
    signed = jnp.where(which == 2 * token, product, jnp.where(which == 2 * token + 1, -product, 0.0))
    step = first * second * jnp.sum(signed, axis=0, keepdims=True)
    pieces = split3((hot0 - hot1) * step)
    earlier = lax.broadcasted_iota(jnp.int32, (rows, rows), 0) < lax.broadcasted_iota(jnp.int32, (rows, rows), 1)
    rank = nn((hot0 + hot1).astype(BF16), earlier.astype(BF16))
    rank0 = jnp.sum(hot0 * rank, axis=0, keepdims=True).astype(jnp.int32)
    rank1 = jnp.sum(hot1 * rank, axis=0, keepdims=True).astype(jnp.int32)
    slot = lax.broadcasted_iota(jnp.int32, (slots, rows), 0)
    slot = (slot // (copies * capacity)) * capacity + slot % capacity
    take0 = slot == e0 * capacity + rank0
    take1 = slot == e1 * capacity + rank1
    gate = jnp.sum(jnp.where(take0, first, 0.0) + jnp.where(take1, second, 0.0), axis=1, keepdims=True)
    pick = (take0 | take1).astype(BF16)
    chunk = 512
    for at in range(0, width, chunk):
        columns = slice(at, at + chunk)
        out_ref[:, columns] = (nn(pick, moe_ref[:, columns]) * gate).astype(BF16)
        table = jnp.concatenate([router_ref[:, columns].astype(F32)] * 3, axis=0).astype(BF16)
        ngrad_ref[:, columns] = lax.dot_general(
            pieces, table, (((0,), (0,)), ((), ())), preferred_element_type=F32
        ).astype(BF16)
        sums = nn(pieces, normed_ref[:, columns])
        rgrad_ref[:, columns] = (
            sums[0:EXPERTS] + sums[EXPERTS:2 * EXPERTS] + sums[2 * EXPERTS:]
        ) * (1.0 / all_tokens)


def on_device(queries, key_heads, value_heads, attn_grad, segments, moe_grad, expert_out, normed, router, routes):
    tok = queries.shape[0]
    ep_size = lax.axis_size("ep")
    inside = jnp.sum((segments[:, None] < segments[None, :]).astype(jnp.int32), axis=0)
    start = (REACH * tok + inside)[None, :]

    moe_rows, width = moe_grad.shape
    capacity = moe_rows * TOP // EXPERTS
    copies = max(1, ep_size // EXPERTS)
    per_device = max(1, EXPERTS // ep_size)
    slots = EXPERTS * copies * capacity
    devices = lax.axis_size("seq") * ep_size
    normed_grad, local_router, outgoing = pl.pallas_call(
        functools.partial(route_kernel, capacity, copies, moe_rows * devices),
        out_shape=(
            jax.ShapeDtypeStruct((moe_rows, width), BF16),
            jax.ShapeDtypeStruct((EXPERTS, width), F32),
            jax.ShapeDtypeStruct((slots, width), BF16),
        ),
        compiler_params=pltpu.CompilerParams(vmem_limit_bytes=VMEM_LIMIT),
        cost_estimate=pl.CostEstimate(flops=8 * slots * moe_rows * width, bytes_accessed=12 * moe_rows * width, transcendentals=0),
        name="routing",
    )(routes.T, moe_grad, expert_out.reshape(TOP * moe_rows, width), normed, router)
    routed_grads = lax.all_to_all(
        outgoing.reshape(ep_size, per_device * capacity, width), "ep", split_axis=0, concat_axis=0, tiled=True
    )
    query_grad, key_grad, value_grad, router_grad = attention(
        start, jnp.broadcast_to(segments[None, :], (8, tok)), queries, attn_grad, key_heads, value_heads, local_router
    )
    return (query_grad, key_grad, value_grad, normed_grad, router_grad, routed_grads)


def solution(mesh):
    return jax.shard_map(
        on_device,
        mesh=mesh,
        in_specs=(
            P("seq", "ep"),
            P("seq", "ep"),
            P("seq", "ep"),
            P("seq", "ep"),
            P("seq"),
            P(("seq", "ep"), None),
            P(("seq", "ep"), None, None),
            P(("seq", "ep"), None),
            P(),
            P(("seq", "ep"), None),
        ),
        out_specs=(
            P("seq", "ep"),
            P("seq", "ep"),
            P("seq", "ep"),
            P(("seq", "ep"), None),
            P(),
            P(("seq", "ep"), None, None),
        ),
        check_vma=False,
    )
```
